32 devices in a mesh: tok: 4 (over z), tile: 4 (over y, core), pair: 2 (over x).
Axes of the slice: x: 2, y: 2, z: 4, core: 2. Of those that a mesh axis runs over, the one named last changes fastest.
Arguments:
- inputs: bfloat16 [4096, 4096], P(('tok', 'pair'), 'tile'), may hold values from -6 to 6
- output_grads: bfloat16 [4096, 4096], P(('tok', 'pair'), 'tile'), may hold values from -0.09375 to 0.09375
- statistics: float32 [16, 2, 1024, 1024], P('tile', 'pair', 'tok'), may hold values from -30 to 43008, as said below
Outputs:
- update: bfloat16 [16, 1024, 1024], P('tile', ('tok', 'pair'))
- new_statistics: float32 [16, 2, 1024, 1024], P('tile', 'pair', 'tok')
The draws below stay inside these ranges and needn't reach their ends.
Inputs may be any that keep to these rules, and one draw needn't show every extreme that they name: `statistics`: for every block and factor the 1024 x 1024 matrix is symmetric and positive definite.
All inputs are finite; a program needn't handle non-finite values. Where the reference program divides by a largest or mean magnitude, that divisor is 1e-20 or more.
Results may differ from the reference program's by a relative error of at most 0.00325.
The reference program's roundings to bfloat16 on the way count: a program that leaves them out, or rounds other values in their place, can miss the bound.
Values may be sent and summed in bfloat16 or wider, within the bound.
A program may use at most 128 MiB of HBM per device.

```python
import jax
import jax.numpy as jnp
from jax import lax

D = 4096
O = 1024
ITERS = 2
NB = 16
TOKENS = 4096


def draw_statistics(key, part):
    base_key = jax.random.fold_in(key, 7)
    noise_key, extra_key, scale_key = jax.random.split(base_key, 3)
    noise_draw = jnp.clip(jax.random.normal(noise_key, (NB, 2, O, O), jnp.float32), -1.7, 1.7)
    log_range = jnp.log(10.0)
    symmetric = (noise_draw + jnp.swapaxes(noise_draw, 2, 3)) * 0.7071
    identity = jnp.eye(O, dtype=jnp.float32)
    off_part = symmetric * (1.0 - identity)
    spread = jnp.sum(jnp.abs(off_part), axis=3)
    extra_diag = jax.random.uniform(extra_key, (NB, 2, O), jnp.float32, 0.25 * O, 0.5 * O)
    diagonal = 1.25 * spread + extra_diag
    matrix = off_part + diagonal[..., None] * identity
    scales = jnp.exp(jax.random.uniform(scale_key, (NB, 2, O), jnp.float32, 0.0, 1.0) * log_range)
    root_scales = jnp.sqrt(scales)
    return 0.1 * root_scales[..., :, None] * matrix * root_scales[..., None, :]


def shard_levels(stream_key, shape, cuts, least, high):
    def one(position, blocks):
        heights = jax.random.uniform(jax.random.fold_in(jax.random.fold_in(stream_key, 6), position), (blocks,), jnp.float32, least / len(cuts), high / len(cuts))
        return jnp.repeat(jnp.exp(heights), shape[position] // blocks).reshape((-1,) + (1,) * (len(shape) - position - 1))

    factor_of = one(*cuts[0])
    for cut in cuts[1:]:
        factor_of = factor_of * one(*cut)
    return factor_of


def gaussian(rng, extent, scale, most, pieces=(), kind=jnp.bfloat16):
    array = scale * jax.random.normal(rng, extent, jnp.float32)
    if pieces:
        array = array * shard_levels(rng, extent, pieces, -0.22, 0.18)
    return jnp.clip(array, -most, most).astype(kind)


def setup_inputs(seed: int = 0) -> dict:
    arg_keys = jax.random.split(jax.random.key(seed), 4)
    return {
        "inputs": gaussian(arg_keys[0], (TOKENS, D), 1.0, 6.0, ((0, 8), (1, 4))),
        "output_grads": gaussian(arg_keys[1], (TOKENS, D), TOKENS ** -0.5, 0.09375, ((0, 8), (1, 4))),
        "statistics": draw_statistics(jax.random.fold_in(arg_keys[3], 71), 0),
    }


def inverse_root(updated):
    identity = jnp.eye(O, dtype=jnp.float32)
    bound_max = jnp.max(lax.optimization_barrier(jnp.sum(jnp.abs(updated), axis=1)))
    iterate = ((updated + 0.1 * bound_max * identity) / (1.1 * bound_max)).astype(jnp.bfloat16)
    iterate = lax.optimization_barrier(iterate)
    root_whole = iterate
    for iteration in range(ITERS):
        factor = ((5.0 * identity - iterate.astype(jnp.float32)) / 4.0).astype(jnp.bfloat16)
        if iteration == 0:
            root_whole = factor
        else:
            root_whole = jnp.dot(root_whole, factor, preferred_element_type=jnp.float32).astype(jnp.bfloat16)
        if iteration + 1 < ITERS:
            square = jnp.dot(factor, factor, preferred_element_type=jnp.float32).astype(jnp.bfloat16)
            fourth = jnp.dot(square, square, preferred_element_type=jnp.float32).astype(jnp.bfloat16)
            iterate = jnp.dot(fourth, iterate, preferred_element_type=jnp.float32).astype(jnp.bfloat16)
            iterate = lax.optimization_barrier(iterate)
    return root_whole

def reference(inputs, output_grads, statistics):
    per_side = D // O

    def block_step(operands):
        block_index, previous = operands
        row_start = (block_index // per_side * O).astype(jnp.int32)
        col_start = (block_index % per_side * O).astype(jnp.int32)
        left_acts = lax.dynamic_slice_in_dim(inputs, row_start, O, 1)
        right_cots = lax.dynamic_slice_in_dim(output_grads, col_start, O, 1)
        gradient = jnp.dot(left_acts.T, right_cots, preferred_element_type=jnp.float32)
        grad_bf = gradient.astype(jnp.bfloat16)
        grad_sq = jnp.sum(jnp.square(grad_bf.astype(jnp.float32)))
        left_stat = 0.9 * previous[0] + 0.1 * jnp.dot(grad_bf, grad_bf.T, preferred_element_type=jnp.float32)
        right_stat = 0.9 * previous[1] + 0.1 * jnp.dot(grad_bf.T, grad_bf, preferred_element_type=jnp.float32)
        left_root = inverse_root(left_stat)
        right_root = inverse_root(right_stat)
        left_mixed = jnp.dot(left_root, grad_bf, preferred_element_type=jnp.float32).astype(jnp.bfloat16)
        raw_update = jnp.dot(left_mixed, right_root, preferred_element_type=jnp.float32)
        update_sq = jnp.sum(raw_update * raw_update)
        updated_block = (raw_update * jnp.sqrt(grad_sq / (update_sq + 1e-06))).astype(jnp.bfloat16)
        return (updated_block, jnp.stack([left_stat, right_stat]))
    updates, new_statistics = lax.map(block_step, (jnp.arange(NB, dtype=jnp.int32), statistics))
    return (updates, new_statistics)
```

```python
import jax
import jax.numpy as jnp
from jax import lax
from jax.sharding import PartitionSpec as P

ITERS = 2


def swapped(shard, axis, stride):
    return lax.ppermute(shard, axis, [(i, i ^ 1 << stride) for i in range(lax.axis_size(axis))])


def product_bf(left_part, right_part):
    return jnp.einsum(
        "kab,kbc->kac", left_part, right_part, preferred_element_type=jnp.float32
    ).astype(jnp.bfloat16)


def general_plan(inputs, output_grads, statistics):
    blocks = statistics.shape[0]
    state_rows = statistics.shape[2]
    matrix_order = statistics.shape[3]
    tile_count = lax.axis_size("tile")
    model_width = inputs.shape[1] * tile_count
    per_side = model_width // matrix_order
    tok_index = lax.axis_index("tok")
    pair_index = lax.axis_index("pair")
    shard_index = tok_index * lax.axis_size("pair") + pair_index
    devices_block = lax.axis_size("tok") * lax.axis_size("pair")
    out_rows = matrix_order // devices_block
    activations, cotangents = (
        lax.all_gather(inputs, "tile", axis=1, tiled=True),
        lax.all_gather(output_grads, "tile", axis=1, tiled=True),
    )
    first_block = lax.axis_index("tile") * blocks
    left_list = []
    right_list = []
    for offset in range(blocks):
        block_id = first_block + offset
        left_list.append(
            lax.dynamic_slice_in_dim(
                activations, block_id // per_side * matrix_order, matrix_order, 1
            )
        )
        right_list.append(
            lax.dynamic_slice_in_dim(
                cotangents, block_id % per_side * matrix_order, matrix_order, 1
            )
        )
    left_acts = jnp.stack(left_list)
    right_cots = jnp.stack(right_list)
    grad_share = lax.psum_scatter(
        jnp.einsum("ktr,ktc->rkc", left_acts, right_cots, preferred_element_type=jnp.float32),
        ("tok", "pair"),
        scatter_dimension=0,
        tiled=True,
    )
    gradient = lax.all_gather(grad_share.astype(jnp.bfloat16), ("tok", "pair"), axis=0, tiled=True)
    grad_sq = jnp.einsum("rkc,rkc->k", gradient, gradient, preferred_element_type=jnp.float32)
    by_rows = jnp.transpose(gradient, (1, 0, 2))
    by_cols = jnp.transpose(gradient, (1, 2, 0))
    factor_data = jnp.where(pair_index == 0, by_rows, by_cols)
    identity = jnp.eye(matrix_order, dtype=jnp.float32)
    row_start = tok_index * state_rows
    previous = lax.all_gather(statistics[:, 0], "tok", axis=1, tiled=True)
    product = jnp.einsum(
        "kac,kbc->kab", factor_data, factor_data, preferred_element_type=jnp.float32
    )
    updated = 0.9 * previous + 0.1 * product
    new_rows = lax.dynamic_slice_in_dim(updated, row_start, state_rows, 1)
    bound_max = jnp.max(jnp.sum(jnp.abs(updated), axis=2), axis=1)[:, None, None]
    iterate = ((updated + 0.1 * bound_max * identity) / (1.1 * bound_max)).astype(jnp.bfloat16)
    iterate = lax.optimization_barrier(iterate)
    root_whole = iterate
    for iteration in range(ITERS):
        factor = ((5.0 * identity - iterate.astype(jnp.float32)) / 4.0).astype(jnp.bfloat16)
        if iteration == 0:
            root_whole = factor
        else:
            root_whole = product_bf(root_whole, factor)
        if iteration + 1 < ITERS:
            square = product_bf(factor, factor)
            fourth = product_bf(square, square)
            iterate = lax.optimization_barrier(product_bf(fourth, iterate))
    partner = swapped(root_whole, "pair", 0)
    left_whole = jnp.where(pair_index == 0, root_whole, partner)
    right_whole = jnp.where(pair_index == 0, partner, root_whole)
    left_part = lax.dynamic_slice_in_dim(left_whole, shard_index * out_rows, out_rows, 1)
    left_mixed = jnp.einsum(
        "kqr,rkc->kqc", left_part, gradient, preferred_element_type=jnp.float32
    ).astype(jnp.bfloat16)
    raw_update = jnp.einsum(
        "kqc,kcd->kqd", left_mixed, right_whole, preferred_element_type=jnp.float32
    )
    local_sq = jnp.sum(raw_update * raw_update, axis=(1, 2))
    update_total = lax.psum(local_sq, ("tok", "pair"))
    graft_ratio = jnp.sqrt(grad_sq / (update_total + 1e-06))
    update = (raw_update * graft_ratio[:, None, None]).astype(jnp.bfloat16)
    return (update, new_rows[:, None])


def dot_bf(left_part, right_part):
    return jnp.dot(left_part, right_part, preferred_element_type=jnp.float32).astype(jnp.bfloat16)


def exchange(pieces, axis):
    size = lax.axis_size(axis)
    index = lax.axis_index(axis)
    result = pieces
    for step in range(1, size):
        piece = lax.dynamic_index_in_dim(pieces, index ^ step, 0, keepdims=True)
        arrived = lax.ppermute(piece, axis, [(i, i ^ step) for i in range(size)])
        result = lax.dynamic_update_slice_in_dim(result, arrived, index ^ step, 0)
    return result


def gather_cotangents(output_grads, tok_size):
    tok_index = lax.axis_index("tok")
    tile_index = lax.axis_index("tile")
    quarters = output_grads.reshape(tok_size, -1, output_grads.shape[1])
    held = jnp.zeros_like(quarters)
    for step in range(tok_size):
        pairs = [
            (tok * tok_size + tile, tile * tok_size + (tok + step) % tok_size)
            for tok in range(tok_size)
            for tile in range(tok_size)
        ]
        piece = lax.dynamic_index_in_dim(quarters, (tok_index + step) % tok_size, 0, keepdims=True)
        arrived = lax.ppermute(piece, ("tok", "tile"), pairs)
        source = (tile_index + tok_size - step) % tok_size
        held = lax.dynamic_update_slice_in_dim(held, arrived, source, 0)
    return lax.all_gather(held, "tile", axis=0)


def owner_plan(inputs, output_grads, statistics):
    blocks, _, state_rows, order = statistics.shape
    tok_index = lax.axis_index("tok")
    pair_index = lax.axis_index("pair")
    half = order // 2
    cots = gather_cotangents(output_grads, blocks)
    acts = lax.all_gather(inputs, "tok", axis=0)
    cots = jnp.swapaxes(cots, 0, 1).reshape(-1, order)
    acts = acts.reshape(-1, order)
    previous = exchange(statistics[:, 0], "tok").reshape(order, order)

    def share(which):
        columns = lax.dynamic_slice_in_dim(acts, which * half, half, 1)
        return lax.dot_general(
            columns, cots, (((0,), (0,)), ((), ())), preferred_element_type=jnp.float32
        )

    theirs = swapped(share(1 - pair_index), "pair", 0)
    mine = (share(pair_index) + theirs).astype(jnp.bfloat16)
    other = swapped(mine, "pair", 0)
    first = pair_index == 0
    gradient = jnp.concatenate([jnp.where(first, mine, other), jnp.where(first, other, mine)], 0)
    wide = gradient.astype(jnp.float32)
    grad_sq = jnp.sum(wide * wide)
    factor_data = jnp.where(first, gradient, gradient.T)
    product = lax.dot_general(
        factor_data, factor_data, (((1,), (1,)), ((), ())), preferred_element_type=jnp.float32
    )
    rows = exchange(product.astype(jnp.bfloat16).reshape(blocks, state_rows, order), "tok")
    new_rows = 0.9 * statistics + 0.1 * rows[:, None].astype(jnp.float32)
    updated = 0.9 * previous + 0.1 * product
    identity = jnp.eye(order, dtype=jnp.float32)
    bound_max = jnp.max(jnp.sum(jnp.abs(updated), axis=1))
    iterate = ((updated + 0.1 * bound_max * identity) / (1.1 * bound_max)).astype(jnp.bfloat16)
    iterate = lax.optimization_barrier(iterate)
    root = iterate
    for iteration in range(ITERS):
        factor = ((5.0 * identity - iterate.astype(jnp.float32)) / 4.0).astype(jnp.bfloat16)
        root = factor if iteration == 0 else dot_bf(root, factor)
        if iteration + 1 < ITERS:
            square = dot_bf(factor, factor)
            fourth = dot_bf(square, square)
            iterate = lax.optimization_barrier(dot_bf(fourth, iterate))
    partner = swapped(root, "pair", 0)
    left = jnp.where(first, root, partner)
    right = jnp.where(first, partner, root)
    left = left.reshape(blocks, 2, -1, order)
    left_rows = lax.dynamic_index_in_dim(left, pair_index, 1, keepdims=False).reshape(-1, order)
    left_mixed = dot_bf(left_rows, gradient)
    raw = jnp.dot(left_mixed, right, preferred_element_type=jnp.float32)
    local_sq = jnp.broadcast_to(jnp.sum(raw * raw), (8, 128))
    update_sq = (local_sq + swapped(local_sq, "pair", 0))[0, 0]
    update = (raw * jnp.sqrt(grad_sq / (update_sq + 1e-06))).astype(jnp.bfloat16)
    return (exchange(update.reshape(blocks, -1, order), "tok"), new_rows)


def per_device(inputs, output_grads, statistics):
    blocks, _, _, order = statistics.shape
    tok_size = lax.axis_size("tok")
    owners = (
        blocks == tok_size
        and tok_size == lax.axis_size("tile")
        and tok_size & (tok_size - 1) == 0
        and lax.axis_size("pair") == 2
        and inputs.shape[1] == order
        and inputs.shape[0] % tok_size == 0
    )
    plan = owner_plan if owners else general_plan
    return plan(inputs, output_grads, statistics)


def solution(mesh):
    placed = (
        P(("tok", "pair"), "tile"),
        P(("tok", "pair"), "tile"),
        P("tile", "pair", "tok", None),
    )
    return jax.shard_map(
        per_device,
        mesh=mesh,
        in_specs=placed,
        out_specs=(P("tile", ("tok", "pair"), None), P("tile", "pair", "tok", None)),
        check_vma=False,
    )
```

```python
import jax
import jax.numpy as jnp
from jax import lax
from jax.sharding import PartitionSpec as P

ITERS = 2


def swapped(shard, axis, stride):
    return lax.ppermute(shard, axis, [(i, i ^ 1 << stride) for i in range(lax.axis_size(axis))])


def product_bf(left_part, right_part):
    return jnp.einsum(
        "kab,kbc->kac", left_part, right_part, preferred_element_type=jnp.float32
    ).astype(jnp.bfloat16)


def general_plan(inputs, output_grads, statistics):
    blocks = statistics.shape[0]
    state_rows = statistics.shape[2]
    matrix_order = statistics.shape[3]
    tile_count = lax.axis_size("tile")
    model_width = inputs.shape[1] * tile_count
    per_side = model_width // matrix_order
    tok_index = lax.axis_index("tok")
    pair_index = lax.axis_index("pair")
    shard_index = tok_index * lax.axis_size("pair") + pair_index
    devices_block = lax.axis_size("tok") * lax.axis_size("pair")
    out_rows = matrix_order // devices_block
    activations, cotangents = (
        lax.all_gather(inputs, "tile", axis=1, tiled=True),
        lax.all_gather(output_grads, "tile", axis=1, tiled=True),
    )
    first_block = lax.axis_index("tile") * blocks
    left_list = []
    right_list = []
    for offset in range(blocks):
        block_id = first_block + offset
        left_list.append(
            lax.dynamic_slice_in_dim(
                activations, block_id // per_side * matrix_order, matrix_order, 1
            )
        )
        right_list.append(
            lax.dynamic_slice_in_dim(
                cotangents, block_id % per_side * matrix_order, matrix_order, 1
            )
        )
    left_acts = jnp.stack(left_list)
    right_cots = jnp.stack(right_list)
    grad_share = lax.psum_scatter(
        jnp.einsum("ktr,ktc->rkc", left_acts, right_cots, preferred_element_type=jnp.float32),
        ("tok", "pair"),
        scatter_dimension=0,
        tiled=True,
    )
    gradient = lax.all_gather(grad_share.astype(jnp.bfloat16), ("tok", "pair"), axis=0, tiled=True)
    grad_sq = jnp.einsum("rkc,rkc->k", gradient, gradient, preferred_element_type=jnp.float32)
    by_rows = jnp.transpose(gradient, (1, 0, 2))
    by_cols = jnp.transpose(gradient, (1, 2, 0))
    factor_data = jnp.where(pair_index == 0, by_rows, by_cols)
    identity = jnp.eye(matrix_order, dtype=jnp.float32)
    row_start = tok_index * state_rows
    previous = lax.all_gather(statistics[:, 0], "tok", axis=1, tiled=True)
    product = jnp.einsum(
        "kac,kbc->kab", factor_data, factor_data, preferred_element_type=jnp.float32
    )
    updated = 0.9 * previous + 0.1 * product
    new_rows = lax.dynamic_slice_in_dim(updated, row_start, state_rows, 1)
    bound_max = jnp.max(jnp.sum(jnp.abs(updated), axis=2), axis=1)[:, None, None]
    iterate = ((updated + 0.1 * bound_max * identity) / (1.1 * bound_max)).astype(jnp.bfloat16)
    iterate = lax.optimization_barrier(iterate)
    root_whole = iterate
    for iteration in range(ITERS):
        factor = ((5.0 * identity - iterate.astype(jnp.float32)) / 4.0).astype(jnp.bfloat16)
        if iteration == 0:
            root_whole = factor
        else:
            root_whole = product_bf(root_whole, factor)
        if iteration + 1 < ITERS:
            square = product_bf(factor, factor)
            fourth = product_bf(square, square)
            iterate = lax.optimization_barrier(product_bf(fourth, iterate))
    partner = swapped(root_whole, "pair", 0)
    left_whole = jnp.where(pair_index == 0, root_whole, partner)
    right_whole = jnp.where(pair_index == 0, partner, root_whole)
    left_part = lax.dynamic_slice_in_dim(left_whole, shard_index * out_rows, out_rows, 1)
    left_mixed = jnp.einsum(
        "kqr,rkc->kqc", left_part, gradient, preferred_element_type=jnp.float32
    ).astype(jnp.bfloat16)
    raw_update = jnp.einsum(
        "kqc,kcd->kqd", left_mixed, right_whole, preferred_element_type=jnp.float32
    )
    local_sq = jnp.sum(raw_update * raw_update, axis=(1, 2))
    update_total = lax.psum(local_sq, ("tok", "pair"))
    graft_ratio = jnp.sqrt(grad_sq / (update_total + 1e-06))
    update = (raw_update * graft_ratio[:, None, None]).astype(jnp.bfloat16)
    return (update, new_rows[:, None])


def dot_bf(left_part, right_part):
    return jnp.dot(left_part, right_part, preferred_element_type=jnp.float32).astype(jnp.bfloat16)


def exchange(pieces, axis):
    size = lax.axis_size(axis)
    index = lax.axis_index(axis)
    result = pieces
    for step in range(1, size):
        piece = lax.dynamic_index_in_dim(pieces, index ^ step, 0, keepdims=True)
        arrived = lax.ppermute(piece, axis, [(i, i ^ step) for i in range(size)])
        result = lax.dynamic_update_slice_in_dim(result, arrived, index ^ step, 0)
    return result


def cotangent_quarter(output_grads, tok_size):
    tok_index = lax.axis_index("tok")
    tile_index = lax.axis_index("tile")
    quarters = output_grads.reshape(tok_size, -1, output_grads.shape[1])
    held = jnp.zeros_like(quarters)
    for step in range(tok_size):
        pairs = [
            (tok * tok_size + tile, tile * tok_size + (tok + step) % tok_size)
            for tok in range(tok_size)
            for tile in range(tok_size)
        ]
        piece = lax.dynamic_index_in_dim(quarters, (tok_index + step) % tok_size, 0, keepdims=True)
        arrived = lax.ppermute(piece, ("tok", "tile"), pairs)
        source = (tile_index + tok_size - step) % tok_size
        held = lax.dynamic_update_slice_in_dim(held, arrived, source, 0)
    return held


def spread_over_tile(piece):
    index = lax.axis_index("tile")
    held = [(index, piece)]
    bit = lax.axis_size("tile").bit_length() - 2
    while bit >= 0:
        held += [(which ^ (1 << bit), swapped(part, "tile", bit)) for which, part in held]
        bit -= 1
    return held


def owner_plan(inputs, output_grads, statistics):
    blocks, _, state_rows, order = statistics.shape
    tok_index = lax.axis_index("tok")
    pair_index = lax.axis_index("pair")
    half = order // 2
    quarter = inputs.shape[0] // blocks
    held = cotangent_quarter(output_grads, blocks)
    acts_mine = lax.dynamic_slice_in_dim(inputs, pair_index * half, half, 1)
    acts_given = lax.dynamic_slice_in_dim(inputs, (1 - pair_index) * half, half, 1)
    acts = jnp.concatenate([acts_mine, swapped(acts_given, "pair", 0)], 0)
    acts, held = lax.optimization_barrier((acts, held))
    acts = lax.all_gather(acts, "tok", axis=0, tiled=True)
    cots = jnp.zeros((blocks, 2, blocks, quarter, order), output_grads.dtype)
    for side, part in enumerate((held, swapped(held, "pair", 0))):
        for which, piece in spread_over_tile(part):
            cots = lax.dynamic_update_slice(cots, piece[:, None, None], (0, side, which, 0, 0))
    cots = cots.reshape(-1, order)

    rows_index = tok_index * state_rows
    local_eye = jnp.arange(order)[None, :] == rows_index + jnp.arange(state_rows)[:, None]
    diagonal = jnp.sum(jnp.where(local_eye[None], statistics[:, 0], 0.0), axis=1)
    remainder = diagonal - lax.reduce_precision(diagonal, 8, 7)
    extra = jnp.broadcast_to(remainder[:, None], (blocks, 16, order))
    pieces = jnp.concatenate([statistics[:, 0], extra], 1).astype(jnp.bfloat16)
    pieces, acts = lax.optimization_barrier((pieces, acts))
    arrived = exchange(pieces, "tok")
    identity = jnp.eye(order, dtype=jnp.float32)
    lost = jnp.sum(arrived[:, state_rows].astype(jnp.float32), axis=0)
    previous = arrived[:, :state_rows].reshape(order, order).astype(jnp.float32)
    previous = previous + identity * lost

    mine = lax.dot_general(
        acts, cots, (((0,), (0,)), ((), ())), preferred_element_type=jnp.float32
    ).astype(jnp.bfloat16)
    other = swapped(mine, "pair", 0)
    first = pair_index == 0
    gradient = jnp.concatenate([jnp.where(first, mine, other), jnp.where(first, other, mine)], 0)
    wide = gradient.astype(jnp.float32)
    grad_sq = jnp.sum(wide * wide)
    factor_data = jnp.where(first, gradient, gradient.T)
    product = lax.dot_general(
        factor_data, factor_data, (((1,), (1,)), ((), ())), preferred_element_type=jnp.float32
    )
    rows = exchange(product.astype(jnp.bfloat16).reshape(blocks, state_rows, order), "tok")
    updated = 0.9 * previous + 0.1 * product
    identity = jnp.eye(order, dtype=jnp.float32)
    bound_max = jnp.max(jnp.sum(jnp.abs(updated), axis=1))
    iterate = ((updated + 0.1 * bound_max * identity) / (1.1 * bound_max)).astype(jnp.bfloat16)
    iterate = lax.optimization_barrier(iterate)
    root = iterate
    for iteration in range(ITERS):
        factor = ((5.0 * identity - iterate.astype(jnp.float32)) / 4.0).astype(jnp.bfloat16)
        root = factor if iteration == 0 else dot_bf(root, factor)
        if iteration + 1 < ITERS:
            square = dot_bf(factor, factor)
            fourth = dot_bf(square, square)
            iterate = lax.optimization_barrier(dot_bf(fourth, iterate))
    root, rows = lax.optimization_barrier((root, rows))
    partner = swapped(root, "pair", 0)
    left = jnp.where(first, root, partner)
    right = jnp.where(first, partner, root)
    left = left.reshape(blocks, 2, -1, order)
    left_rows = lax.dynamic_index_in_dim(left, pair_index, 1, keepdims=False).reshape(-1, order)
    left_mixed = dot_bf(left_rows, gradient)
    raw = jnp.dot(left_mixed, right, preferred_element_type=jnp.float32)
    local_sq = jnp.broadcast_to(jnp.sum(raw * raw), (8, 128))
    update_sq = (local_sq + swapped(local_sq, "pair", 0))[0, 0]
    update = (raw * jnp.sqrt(grad_sq / (update_sq + 1e-06))).astype(jnp.bfloat16)
    new_rows = 0.9 * statistics + 0.1 * rows[:, None].astype(jnp.float32)
    return (exchange(update.reshape(blocks, -1, order), "tok"), new_rows)


def per_device(inputs, output_grads, statistics):
    blocks, _, _, order = statistics.shape
    tok_size = lax.axis_size("tok")
    owners = (
        blocks == tok_size
        and tok_size == lax.axis_size("tile")
        and tok_size & (tok_size - 1) == 0
        and lax.axis_size("pair") == 2
        and inputs.shape[1] == order
        and inputs.shape[0] % tok_size == 0
    )
    plan = owner_plan if owners else general_plan
    return plan(inputs, output_grads, statistics)


def solution(mesh):
    placed = (
        P(("tok", "pair"), "tile"),
        P(("tok", "pair"), "tile"),
        P("tile", "pair", "tok", None),
    )
    return jax.shard_map(
        per_device,
        mesh=mesh,
        in_specs=placed,
        out_specs=(P("tile", ("tok", "pair"), None), P("tile", "pair", "tok", None)),
        check_vma=False,
    )
```

```python
import jax
import jax.numpy as jnp
from jax import lax
from jax.sharding import PartitionSpec as P

ITERS = 2


def swapped(shard, axis, stride):
    return lax.ppermute(shard, axis, [(i, i ^ 1 << stride) for i in range(lax.axis_size(axis))])


def product_bf(left_part, right_part):
    return jnp.einsum(
        "kab,kbc->kac", left_part, right_part, preferred_element_type=jnp.float32
    ).astype(jnp.bfloat16)


def general_plan(inputs, output_grads, statistics):
    blocks = statistics.shape[0]
    state_rows = statistics.shape[2]
    matrix_order = statistics.shape[3]
    tile_count = lax.axis_size("tile")
    model_width = inputs.shape[1] * tile_count
    per_side = model_width // matrix_order
    tok_index = lax.axis_index("tok")
    pair_index = lax.axis_index("pair")
    shard_index = tok_index * lax.axis_size("pair") + pair_index
    devices_block = lax.axis_size("tok") * lax.axis_size("pair")
    out_rows = matrix_order // devices_block
    activations, cotangents = (
        lax.all_gather(inputs, "tile", axis=1, tiled=True),
        lax.all_gather(output_grads, "tile", axis=1, tiled=True),
    )
    first_block = lax.axis_index("tile") * blocks
    left_list = []
    right_list = []
    for offset in range(blocks):
        block_id = first_block + offset
        left_list.append(
            lax.dynamic_slice_in_dim(
                activations, block_id // per_side * matrix_order, matrix_order, 1
            )
        )
        right_list.append(
            lax.dynamic_slice_in_dim(
                cotangents, block_id % per_side * matrix_order, matrix_order, 1
            )
        )
    left_acts = jnp.stack(left_list)
    right_cots = jnp.stack(right_list)
    grad_share = lax.psum_scatter(
        jnp.einsum("ktr,ktc->rkc", left_acts, right_cots, preferred_element_type=jnp.float32),
        ("tok", "pair"),
        scatter_dimension=0,
        tiled=True,
    )
    gradient = lax.all_gather(grad_share.astype(jnp.bfloat16), ("tok", "pair"), axis=0, tiled=True)
    grad_sq = jnp.einsum("rkc,rkc->k", gradient, gradient, preferred_element_type=jnp.float32)
    by_rows = jnp.transpose(gradient, (1, 0, 2))
    by_cols = jnp.transpose(gradient, (1, 2, 0))
    factor_data = jnp.where(pair_index == 0, by_rows, by_cols)
    identity = jnp.eye(matrix_order, dtype=jnp.float32)
    row_start = tok_index * state_rows
    previous = lax.all_gather(statistics[:, 0], "tok", axis=1, tiled=True)
    product = jnp.einsum(
        "kac,kbc->kab", factor_data, factor_data, preferred_element_type=jnp.float32
    )
    updated = 0.9 * previous + 0.1 * product
    new_rows = lax.dynamic_slice_in_dim(updated, row_start, state_rows, 1)
    bound_max = jnp.max(jnp.sum(jnp.abs(updated), axis=2), axis=1)[:, None, None]
    iterate = ((updated + 0.1 * bound_max * identity) / (1.1 * bound_max)).astype(jnp.bfloat16)
    iterate = lax.optimization_barrier(iterate)
    root_whole = iterate
    for iteration in range(ITERS):
        factor = ((5.0 * identity - iterate.astype(jnp.float32)) / 4.0).astype(jnp.bfloat16)
        if iteration == 0:
            root_whole = factor
        else:
            root_whole = product_bf(root_whole, factor)
        if iteration + 1 < ITERS:
            square = product_bf(factor, factor)
            fourth = product_bf(square, square)
            iterate = lax.optimization_barrier(product_bf(fourth, iterate))
    partner = swapped(root_whole, "pair", 0)
    left_whole = jnp.where(pair_index == 0, root_whole, partner)
    right_whole = jnp.where(pair_index == 0, partner, root_whole)
    left_part = lax.dynamic_slice_in_dim(left_whole, shard_index * out_rows, out_rows, 1)
    left_mixed = jnp.einsum(
        "kqr,rkc->kqc", left_part, gradient, preferred_element_type=jnp.float32
    ).astype(jnp.bfloat16)
    raw_update = jnp.einsum(
        "kqc,kcd->kqd", left_mixed, right_whole, preferred_element_type=jnp.float32
    )
    local_sq = jnp.sum(raw_update * raw_update, axis=(1, 2))
    update_total = lax.psum(local_sq, ("tok", "pair"))
    graft_ratio = jnp.sqrt(grad_sq / (update_total + 1e-06))
    update = (raw_update * graft_ratio[:, None, None]).astype(jnp.bfloat16)
    return (update, new_rows[:, None])


def dot_bf(left_part, right_part):
    return jnp.dot(left_part, right_part, preferred_element_type=jnp.float32).astype(jnp.bfloat16)


def exchange(pieces, axis):
    size = lax.axis_size(axis)
    index = lax.axis_index(axis)
    result = pieces
    for step in range(1, size):
        piece = lax.dynamic_index_in_dim(pieces, index ^ step, 0, keepdims=True)
        arrived = lax.ppermute(piece, axis, [(i, i ^ step) for i in range(size)])
        result = lax.dynamic_update_slice_in_dim(result, arrived, index ^ step, 0)
    return result


def cotangent_quarter(output_grads, tok_size):
    tok_index = lax.axis_index("tok")
    tile_index = lax.axis_index("tile")
    quarters = output_grads.reshape(tok_size, -1, output_grads.shape[1])
    held = jnp.zeros_like(quarters)
    for step in range(tok_size):
        pairs = [
            (tok * tok_size + tile, tile * tok_size + (tok + step) % tok_size)
            for tok in range(tok_size)
            for tile in range(tok_size)
        ]
        piece = lax.dynamic_index_in_dim(quarters, (tok_index + step) % tok_size, 0, keepdims=True)
        arrived = lax.ppermute(piece, ("tok", "tile"), pairs)
        source = (tile_index + tok_size - step) % tok_size
        held = lax.dynamic_update_slice_in_dim(held, arrived, source, 0)
    return held


def spread_over_tile(piece):
    index = lax.axis_index("tile")
    held = [(index, piece)]
    bit = lax.axis_size("tile").bit_length() - 2
    while bit >= 0:
        held += [(which ^ (1 << bit), swapped(part, "tile", bit)) for which, part in held]
        bit -= 1
    return held


def owner_plan(inputs, output_grads, statistics):
    blocks, _, state_rows, order = statistics.shape
    tok_index = lax.axis_index("tok")
    pair_index = lax.axis_index("pair")
    half = order // 2
    quarter = inputs.shape[0] // blocks
    held = cotangent_quarter(output_grads, blocks)
    acts_mine = lax.dynamic_slice_in_dim(inputs, pair_index * half, half, 1)
    acts_given = lax.dynamic_slice_in_dim(inputs, (1 - pair_index) * half, half, 1)
    acts = jnp.concatenate([acts_mine, swapped(acts_given, "pair", 0)], 0)
    acts, held = lax.optimization_barrier((acts, held))
    acts = lax.all_gather(acts, "tok", axis=0, tiled=True)
    cots = jnp.zeros((blocks, 2, blocks, quarter, order), output_grads.dtype)
    for side, part in enumerate((held, swapped(held, "pair", 0))):
        for which, piece in spread_over_tile(part):
            cots = lax.dynamic_update_slice(cots, piece[:, None, None], (0, side, which, 0, 0))
    cots = cots.reshape(-1, order)

    rows_index = tok_index * state_rows
    local_eye = jnp.arange(order)[None, :] == rows_index + jnp.arange(state_rows)[:, None]
    diagonal = jnp.sum(jnp.where(local_eye[None], statistics[:, 0], 0.0), axis=1)
    remainder = diagonal - lax.reduce_precision(diagonal, 8, 7)
    extra = jnp.broadcast_to(remainder[:, None], (blocks, 16, order))
    pieces = jnp.concatenate([statistics[:, 0], extra], 1).astype(jnp.bfloat16)
    pieces, acts = lax.optimization_barrier((pieces, acts))
    arrived = exchange(pieces, "tok")
    identity = jnp.eye(order, dtype=jnp.float32)
    lost = jnp.sum(arrived[:, state_rows].astype(jnp.float32), axis=0)
    previous = arrived[:, :state_rows].reshape(order, order).astype(jnp.float32)
    previous = previous + identity * lost

    mine = lax.dot_general(
        acts, cots, (((0,), (0,)), ((), ())), preferred_element_type=jnp.float32
    ).astype(jnp.bfloat16)
    other = swapped(mine, "pair", 0)
    first = pair_index == 0
    gradient = jnp.concatenate([jnp.where(first, mine, other), jnp.where(first, other, mine)], 0)
    wide = gradient.astype(jnp.float32)
    grad_sq = jnp.sum(wide * wide)
    factor_data = jnp.where(first, gradient, gradient.T)
    product = lax.dot_general(
        factor_data, factor_data, (((1,), (1,)), ((), ())), preferred_element_type=jnp.float32
    )
    product = lax.optimization_barrier(product)
    rows = exchange(product.astype(jnp.bfloat16).reshape(blocks, state_rows, order), "tok")
    updated = 0.9 * previous + 0.1 * product
    identity = jnp.eye(order, dtype=jnp.float32)
    bound_max = jnp.max(jnp.sum(jnp.abs(updated), axis=1))
    iterate = ((updated + 0.1 * bound_max * identity) / (1.1 * bound_max)).astype(jnp.bfloat16)
    iterate = lax.optimization_barrier(iterate)
    root = iterate
    for iteration in range(ITERS):
        factor = ((5.0 * identity - iterate.astype(jnp.float32)) / 4.0).astype(jnp.bfloat16)
        root = factor if iteration == 0 else dot_bf(root, factor)
        if iteration + 1 < ITERS:
            square = dot_bf(factor, factor)
            fourth = dot_bf(square, square)
            fourth, rows = lax.optimization_barrier((fourth, rows))
            iterate = lax.optimization_barrier(dot_bf(fourth, iterate))
    partner = swapped(root, "pair", 0)
    left = jnp.where(first, root, partner)
    right = jnp.where(first, partner, root)
    left = left.reshape(blocks, 2, -1, order)
    left_rows = lax.dynamic_index_in_dim(left, pair_index, 1, keepdims=False).reshape(-1, order)
    left_mixed = dot_bf(left_rows, gradient)
    raw = jnp.dot(left_mixed, right, preferred_element_type=jnp.float32)
    local_sq = jnp.broadcast_to(jnp.sum(raw * raw), (8, 128))
    update_sq = (local_sq + swapped(local_sq, "pair", 0))[0, 0]
    update = (raw * jnp.sqrt(grad_sq / (update_sq + 1e-06))).astype(jnp.bfloat16)
    new_rows = 0.9 * statistics + 0.1 * rows[:, None].astype(jnp.float32)
    return (exchange(update.reshape(blocks, -1, order), "tok"), new_rows)


def per_device(inputs, output_grads, statistics):
    blocks, _, _, order = statistics.shape
    tok_size = lax.axis_size("tok")
    owners = (
        blocks == tok_size
        and tok_size == lax.axis_size("tile")
        and tok_size & (tok_size - 1) == 0
        and lax.axis_size("pair") == 2
        and inputs.shape[1] == order
        and inputs.shape[0] % tok_size == 0
    )
    plan = owner_plan if owners else general_plan
    return plan(inputs, output_grads, statistics)


def solution(mesh):
    placed = (
        P(("tok", "pair"), "tile"),
        P(("tok", "pair"), "tile"),
        P("tile", "pair", "tok", None),
    )
    return jax.shard_map(
        per_device,
        mesh=mesh,
        in_specs=placed,
        out_specs=(P("tile", ("tok", "pair"), None), P("tile", "pair", "tok", None)),
        check_vma=False,
    )
```

```python
import jax
import jax.numpy as jnp
from jax import lax
from jax.sharding import PartitionSpec as P

ITERS = 2


def swapped(shard, axis, stride):
    return lax.ppermute(shard, axis, [(i, i ^ 1 << stride) for i in range(lax.axis_size(axis))])


def product_bf(left_part, right_part):
    return jnp.einsum(
        "kab,kbc->kac", left_part, right_part, preferred_element_type=jnp.float32
    ).astype(jnp.bfloat16)


def general_plan(inputs, output_grads, statistics):
    blocks = statistics.shape[0]
    state_rows = statistics.shape[2]
    matrix_order = statistics.shape[3]
    tile_count = lax.axis_size("tile")
    model_width = inputs.shape[1] * tile_count
    per_side = model_width // matrix_order
    tok_index = lax.axis_index("tok")
    pair_index = lax.axis_index("pair")
    shard_index = tok_index * lax.axis_size("pair") + pair_index
    devices_block = lax.axis_size("tok") * lax.axis_size("pair")
    out_rows = matrix_order // devices_block
    activations, cotangents = (
        lax.all_gather(inputs, "tile", axis=1, tiled=True),
        lax.all_gather(output_grads, "tile", axis=1, tiled=True),
    )
    first_block = lax.axis_index("tile") * blocks
    left_list = []
    right_list = []
    for offset in range(blocks):
        block_id = first_block + offset
        left_list.append(
            lax.dynamic_slice_in_dim(
                activations, block_id // per_side * matrix_order, matrix_order, 1
            )
        )
        right_list.append(
            lax.dynamic_slice_in_dim(
                cotangents, block_id % per_side * matrix_order, matrix_order, 1
            )
        )
    left_acts = jnp.stack(left_list)
    right_cots = jnp.stack(right_list)
    grad_share = lax.psum_scatter(
        jnp.einsum("ktr,ktc->rkc", left_acts, right_cots, preferred_element_type=jnp.float32),
        ("tok", "pair"),
        scatter_dimension=0,
        tiled=True,
    )
    gradient = lax.all_gather(grad_share.astype(jnp.bfloat16), ("tok", "pair"), axis=0, tiled=True)
    grad_sq = jnp.einsum("rkc,rkc->k", gradient, gradient, preferred_element_type=jnp.float32)
    by_rows = jnp.transpose(gradient, (1, 0, 2))
    by_cols = jnp.transpose(gradient, (1, 2, 0))
    factor_data = jnp.where(pair_index == 0, by_rows, by_cols)
    identity = jnp.eye(matrix_order, dtype=jnp.float32)
    row_start = tok_index * state_rows
    previous = lax.all_gather(statistics[:, 0], "tok", axis=1, tiled=True)
    product = jnp.einsum(
        "kac,kbc->kab", factor_data, factor_data, preferred_element_type=jnp.float32
    )
    updated = 0.9 * previous + 0.1 * product
    new_rows = lax.dynamic_slice_in_dim(updated, row_start, state_rows, 1)
    bound_max = jnp.max(jnp.sum(jnp.abs(updated), axis=2), axis=1)[:, None, None]
    iterate = ((updated + 0.1 * bound_max * identity) / (1.1 * bound_max)).astype(jnp.bfloat16)
    iterate = lax.optimization_barrier(iterate)
    root_whole = iterate
    for iteration in range(ITERS):
        factor = ((5.0 * identity - iterate.astype(jnp.float32)) / 4.0).astype(jnp.bfloat16)
        if iteration == 0:
            root_whole = factor
        else:
            root_whole = product_bf(root_whole, factor)
        if iteration + 1 < ITERS:
            square = product_bf(factor, factor)
            fourth = product_bf(square, square)
            iterate = lax.optimization_barrier(product_bf(fourth, iterate))
    partner = swapped(root_whole, "pair", 0)
    left_whole = jnp.where(pair_index == 0, root_whole, partner)
    right_whole = jnp.where(pair_index == 0, partner, root_whole)
    left_part = lax.dynamic_slice_in_dim(left_whole, shard_index * out_rows, out_rows, 1)
    left_mixed = jnp.einsum(
        "kqr,rkc->kqc", left_part, gradient, preferred_element_type=jnp.float32
    ).astype(jnp.bfloat16)
    raw_update = jnp.einsum(
        "kqc,kcd->kqd", left_mixed, right_whole, preferred_element_type=jnp.float32
    )
    local_sq = jnp.sum(raw_update * raw_update, axis=(1, 2))
    update_total = lax.psum(local_sq, ("tok", "pair"))
    graft_ratio = jnp.sqrt(grad_sq / (update_total + 1e-06))
    update = (raw_update * graft_ratio[:, None, None]).astype(jnp.bfloat16)
    return (update, new_rows[:, None])


def dot_bf(left_part, right_part):
    return jnp.dot(left_part, right_part, preferred_element_type=jnp.float32).astype(jnp.bfloat16)


def exchange(pieces, axis):
    size = lax.axis_size(axis)
    index = lax.axis_index(axis)
    result = pieces
    for step in range(1, size):
        piece = lax.dynamic_index_in_dim(pieces, index ^ step, 0, keepdims=True)
        arrived = lax.ppermute(piece, axis, [(i, i ^ step) for i in range(size)])
        result = lax.dynamic_update_slice_in_dim(result, arrived, index ^ step, 0)
    return result


def cotangent_quarter(output_grads, tok_size):
    tok_index = lax.axis_index("tok")
    tile_index = lax.axis_index("tile")
    quarters = output_grads.reshape(tok_size, -1, output_grads.shape[1])
    held = jnp.zeros_like(quarters)
    for step in range(tok_size):
        pairs = [
            (tok * tok_size + tile, tile * tok_size + (tok + step) % tok_size)
            for tok in range(tok_size)
            for tile in range(tok_size)
        ]
        piece = lax.dynamic_index_in_dim(quarters, (tok_index + step) % tok_size, 0, keepdims=True)
        arrived = lax.ppermute(piece, ("tok", "tile"), pairs)
        source = (tile_index + tok_size - step) % tok_size
        held = lax.dynamic_update_slice_in_dim(held, arrived, source, 0)
    return held


def spread_over_tile(piece):
    index = lax.axis_index("tile")
    held = [(index, piece)]
    bit = lax.axis_size("tile").bit_length() - 2
    while bit >= 0:
        held += [(which ^ (1 << bit), swapped(part, "tile", bit)) for which, part in held]
        bit -= 1
    return held


def owner_plan(inputs, output_grads, statistics):
    blocks, _, state_rows, order = statistics.shape
    tok_index = lax.axis_index("tok")
    pair_index = lax.axis_index("pair")
    half = order // 2
    quarter = inputs.shape[0] // blocks
    held = cotangent_quarter(output_grads, blocks)
    acts_mine = lax.dynamic_slice_in_dim(inputs, pair_index * half, half, 1)
    acts_given = lax.dynamic_slice_in_dim(inputs, (1 - pair_index) * half, half, 1)
    acts = jnp.concatenate([acts_mine, swapped(acts_given, "pair", 0)], 0)
    acts, held = lax.optimization_barrier((acts, held))
    acts = lax.all_gather(acts, "tok", axis=0, tiled=True)
    cots = jnp.zeros((blocks, 2, blocks, quarter, order), output_grads.dtype)
    for side, part in enumerate((held, swapped(held, "pair", 0))):
        for which, piece in spread_over_tile(part):
            cots = lax.dynamic_update_slice(cots, piece[:, None, None], (0, side, which, 0, 0))
    cots = cots.reshape(-1, order)

    rows_index = tok_index * state_rows
    local_eye = jnp.arange(order)[None, :] == rows_index + jnp.arange(state_rows)[:, None]
    diagonal = jnp.sum(jnp.where(local_eye[None], statistics[:, 0], 0.0), axis=1)
    remainder = diagonal - lax.reduce_precision(diagonal, 8, 7)
    extra = jnp.broadcast_to(remainder[:, None], (blocks, 16, order))
    pieces = jnp.concatenate([statistics[:, 0], extra], 1).astype(jnp.bfloat16)
    pieces, acts = lax.optimization_barrier((pieces, acts))
    arrived = exchange(pieces, "tok")
    identity = jnp.eye(order, dtype=jnp.float32)
    lost = jnp.sum(arrived[:, state_rows].astype(jnp.float32), axis=0)
    previous = arrived[:, :state_rows].reshape(order, order).astype(jnp.float32)
    previous = previous + identity * lost

    mine = lax.dot_general(
        acts, cots, (((0,), (0,)), ((), ())), preferred_element_type=jnp.float32
    ).astype(jnp.bfloat16)
    other = swapped(mine, "pair", 0)
    first = pair_index == 0
    gradient = jnp.concatenate([jnp.where(first, mine, other), jnp.where(first, other, mine)], 0)
    wide = gradient.astype(jnp.float32)
    grad_sq = jnp.sum(wide * wide)
    factor_data = jnp.where(first, gradient, gradient.T)
    product = lax.dot_general(
        factor_data, factor_data, (((1,), (1,)), ((), ())), preferred_element_type=jnp.float32
    )
    product = lax.optimization_barrier(product)
    rows = exchange(product.astype(jnp.bfloat16).reshape(blocks, state_rows, order), "tok")
    updated = 0.9 * previous + 0.1 * product
    identity = jnp.eye(order, dtype=jnp.float32)
    bound_max = jnp.max(jnp.sum(jnp.abs(updated), axis=1))
    iterate = ((updated + 0.1 * bound_max * identity) / (1.1 * bound_max)).astype(jnp.bfloat16)
    iterate = lax.optimization_barrier(iterate)
    root = iterate
    for iteration in range(ITERS):
        factor = ((5.0 * identity - iterate.astype(jnp.float32)) / 4.0).astype(jnp.bfloat16)
        root = factor if iteration == 0 else dot_bf(root, factor)
        if iteration + 1 < ITERS:
            square = dot_bf(factor, factor)
            fourth = dot_bf(square, square)
            iterate = lax.optimization_barrier(dot_bf(fourth, iterate))
    partner = swapped(root, "pair", 0)
    partner, rows = lax.optimization_barrier((partner, rows))
    left = jnp.where(first, root, partner)
    right = jnp.where(first, partner, root)
    left = left.reshape(blocks, 2, -1, order)
    left_rows = lax.dynamic_index_in_dim(left, pair_index, 1, keepdims=False).reshape(-1, order)
    left_mixed = dot_bf(left_rows, gradient)
    raw = jnp.dot(left_mixed, right, preferred_element_type=jnp.float32)
    local_sq = jnp.broadcast_to(jnp.sum(raw * raw), (8, 128))
    update_sq = (local_sq + swapped(local_sq, "pair", 0))[0, 0]
    update = (raw * jnp.sqrt(grad_sq / (update_sq + 1e-06))).astype(jnp.bfloat16)
    new_rows = 0.9 * statistics + 0.1 * rows[:, None].astype(jnp.float32)
    return (exchange(update.reshape(blocks, -1, order), "tok"), new_rows)


def per_device(inputs, output_grads, statistics):
    blocks, _, _, order = statistics.shape
    tok_size = lax.axis_size("tok")
    owners = (
        blocks == tok_size
        and tok_size == lax.axis_size("tile")
        and tok_size & (tok_size - 1) == 0
        and lax.axis_size("pair") == 2
        and inputs.shape[1] == order
        and inputs.shape[0] % tok_size == 0
    )
    plan = owner_plan if owners else general_plan
    return plan(inputs, output_grads, statistics)


def solution(mesh):
    placed = (
        P(("tok", "pair"), "tile"),
        P(("tok", "pair"), "tile"),
        P("tile", "pair", "tok", None),
    )
    return jax.shard_map(
        per_device,
        mesh=mesh,
        in_specs=placed,
        out_specs=(P("tile", ("tok", "pair"), None), P("tile", "pair", "tok", None)),
        check_vma=False,
    )
```

```python
import functools

import jax
import jax.numpy as jnp
from jax import lax
from jax.experimental import pallas as pl
from jax.experimental.pallas import tpu as pltpu
from jax.sharding import PartitionSpec as P

ITERS = 2


def swapped(shard, axis, stride):
    return lax.ppermute(shard, axis, [(i, i ^ 1 << stride) for i in range(lax.axis_size(axis))])


def product_bf(left_part, right_part):
    return jnp.einsum(
        "kab,kbc->kac", left_part, right_part, preferred_element_type=jnp.float32
    ).astype(jnp.bfloat16)


def general_plan(inputs, output_grads, statistics):
    blocks = statistics.shape[0]
    state_rows = statistics.shape[2]
    matrix_order = statistics.shape[3]
    tile_count = lax.axis_size("tile")
    model_width = inputs.shape[1] * tile_count
    per_side = model_width // matrix_order
    tok_index = lax.axis_index("tok")
    pair_index = lax.axis_index("pair")
    shard_index = tok_index * lax.axis_size("pair") + pair_index
    devices_block = lax.axis_size("tok") * lax.axis_size("pair")
    out_rows = matrix_order // devices_block
    activations, cotangents = (
        lax.all_gather(inputs, "tile", axis=1, tiled=True),
        lax.all_gather(output_grads, "tile", axis=1, tiled=True),
    )
    first_block = lax.axis_index("tile") * blocks
    left_list = []
    right_list = []
    for offset in range(blocks):
        block_id = first_block + offset
        left_list.append(
            lax.dynamic_slice_in_dim(
                activations, block_id // per_side * matrix_order, matrix_order, 1
            )
        )
        right_list.append(
            lax.dynamic_slice_in_dim(
                cotangents, block_id % per_side * matrix_order, matrix_order, 1
            )
        )
    left_acts = jnp.stack(left_list)
    right_cots = jnp.stack(right_list)
    grad_share = lax.psum_scatter(
        jnp.einsum("ktr,ktc->rkc", left_acts, right_cots, preferred_element_type=jnp.float32),
        ("tok", "pair"),
        scatter_dimension=0,
        tiled=True,
    )
    gradient = lax.all_gather(grad_share.astype(jnp.bfloat16), ("tok", "pair"), axis=0, tiled=True)
    grad_sq = jnp.einsum("rkc,rkc->k", gradient, gradient, preferred_element_type=jnp.float32)
    by_rows = jnp.transpose(gradient, (1, 0, 2))
    by_cols = jnp.transpose(gradient, (1, 2, 0))
    factor_data = jnp.where(pair_index == 0, by_rows, by_cols)
    identity = jnp.eye(matrix_order, dtype=jnp.float32)
    row_start = tok_index * state_rows
    previous = lax.all_gather(statistics[:, 0], "tok", axis=1, tiled=True)
    product = jnp.einsum(
        "kac,kbc->kab", factor_data, factor_data, preferred_element_type=jnp.float32
    )
    updated = 0.9 * previous + 0.1 * product
    new_rows = lax.dynamic_slice_in_dim(updated, row_start, state_rows, 1)
    bound_max = jnp.max(jnp.sum(jnp.abs(updated), axis=2), axis=1)[:, None, None]
    iterate = ((updated + 0.1 * bound_max * identity) / (1.1 * bound_max)).astype(jnp.bfloat16)
    iterate = lax.optimization_barrier(iterate)
    root_whole = iterate
    for iteration in range(ITERS):
        factor = ((5.0 * identity - iterate.astype(jnp.float32)) / 4.0).astype(jnp.bfloat16)
        if iteration == 0:
            root_whole = factor
        else:
            root_whole = product_bf(root_whole, factor)
        if iteration + 1 < ITERS:
            square = product_bf(factor, factor)
            fourth = product_bf(square, square)
            iterate = lax.optimization_barrier(product_bf(fourth, iterate))
    partner = swapped(root_whole, "pair", 0)
    left_whole = jnp.where(pair_index == 0, root_whole, partner)
    right_whole = jnp.where(pair_index == 0, partner, root_whole)
    left_part = lax.dynamic_slice_in_dim(left_whole, shard_index * out_rows, out_rows, 1)
    left_mixed = jnp.einsum(
        "kqr,rkc->kqc", left_part, gradient, preferred_element_type=jnp.float32
    ).astype(jnp.bfloat16)
    raw_update = jnp.einsum(
        "kqc,kcd->kqd", left_mixed, right_whole, preferred_element_type=jnp.float32
    )
    local_sq = jnp.sum(raw_update * raw_update, axis=(1, 2))
    update_total = lax.psum(local_sq, ("tok", "pair"))
    graft_ratio = jnp.sqrt(grad_sq / (update_total + 1e-06))
    update = (raw_update * graft_ratio[:, None, None]).astype(jnp.bfloat16)
    return (update, new_rows[:, None])


def dot_bf(left_part, right_part):
    return jnp.dot(left_part, right_part, preferred_element_type=jnp.float32).astype(jnp.bfloat16)


def exchange(pieces, axis):
    size = lax.axis_size(axis)
    index = lax.axis_index(axis)
    result = pieces
    for step in range(1, size):
        piece = lax.dynamic_index_in_dim(pieces, index ^ step, 0, keepdims=True)
        arrived = lax.ppermute(piece, axis, [(i, i ^ step) for i in range(size)])
        result = lax.dynamic_update_slice_in_dim(result, arrived, index ^ step, 0)
    return result


def cotangent_quarter(output_grads, tok_size):
    tok_index = lax.axis_index("tok")
    tile_index = lax.axis_index("tile")
    quarters = output_grads.reshape(tok_size, -1, output_grads.shape[1])
    held = jnp.zeros_like(quarters)
    for step in range(tok_size):
        pairs = [
            (tok * tok_size + tile, tile * tok_size + (tok + step) % tok_size)
            for tok in range(tok_size)
            for tile in range(tok_size)
        ]
        piece = lax.dynamic_index_in_dim(quarters, (tok_index + step) % tok_size, 0, keepdims=True)
        arrived = lax.ppermute(piece, ("tok", "tile"), pairs)
        source = (tile_index + tok_size - step) % tok_size
        held = lax.dynamic_update_slice_in_dim(held, arrived, source, 0)
    return held


def spread_over_tile(piece):
    index = lax.axis_index("tile")
    held = [(index, piece)]
    bit = lax.axis_size("tile").bit_length() - 2
    while bit >= 0:
        held += [(which ^ (1 << bit), swapped(part, "tile", bit)) for which, part in held]
        bit -= 1
    return held


def transfer_body(size, with_swap, *refs):
    if with_swap:
        pieces, whole, result, partner, send_sem, recv_sem, own_sem = refs
    else:
        pieces, result, send_sem, recv_sem, own_sem = refs
    me = lax.axis_index("tok")
    side = lax.axis_index("pair")
    targets = [{"tok": lax.rem(me + step, size)} for step in range(1, size)]
    if with_swap:
        targets.append({"pair": 1 - side})
    barrier = pltpu.get_barrier_semaphore()
    for target in targets:
        pl.semaphore_signal(barrier, inc=1, device_id=target, device_id_type=pl.DeviceIdType.MESH)
    pl.semaphore_wait(barrier, len(targets))
    copies = []
    for slot, target in enumerate(targets):
        to_pair = slot == size - 1
        copies.append(
            pltpu.make_async_remote_copy(
                src_ref=whole if to_pair else pieces.at[target["tok"]],
                dst_ref=partner if to_pair else result.at[me],
                send_sem=send_sem.at[slot],
                recv_sem=recv_sem.at[slot],
                device_id=target,
                device_id_type=pl.DeviceIdType.MESH,
            )
        )
        copies[-1].start()
    own = pltpu.make_async_copy(pieces.at[me], result.at[me], own_sem)
    own.start()
    own.wait()
    for copy in copies:
        copy.wait()


def transfer(pieces, whole, collective_id):
    size = lax.axis_size("tok")
    arrays = [pieces] if whole is None else [pieces, whole]
    slots = size - 1 + (whole is not None)
    anywhere = pl.BlockSpec(memory_space=pl.ANY)
    return pl.pallas_call(
        functools.partial(transfer_body, size, whole is not None),
        out_shape=[jax.ShapeDtypeStruct(array.shape, array.dtype) for array in arrays],
        in_specs=[anywhere] * len(arrays),
        out_specs=[anywhere] * len(arrays),
        scratch_shapes=[
            pltpu.SemaphoreType.DMA((slots,)),
            pltpu.SemaphoreType.DMA((slots,)),
            pltpu.SemaphoreType.DMA,
        ],
        compiler_params=pltpu.CompilerParams(collective_id=collective_id, has_side_effects=True),
    )(*arrays)


def owner_plan(inputs, output_grads, statistics):
    blocks, _, state_rows, order = statistics.shape
    tok_index = lax.axis_index("tok")
    pair_index = lax.axis_index("pair")
    half = order // 2
    quarter = inputs.shape[0] // blocks
    held = cotangent_quarter(output_grads, blocks)
    acts_mine = lax.dynamic_slice_in_dim(inputs, pair_index * half, half, 1)
    acts_given = lax.dynamic_slice_in_dim(inputs, (1 - pair_index) * half, half, 1)
    acts = jnp.concatenate([acts_mine, swapped(acts_given, "pair", 0)], 0)
    acts, held = lax.optimization_barrier((acts, held))
    acts = lax.all_gather(acts, "tok", axis=0, tiled=True)
    cots = jnp.zeros((blocks, 2, blocks, quarter, order), output_grads.dtype)
    for side, part in enumerate((held, swapped(held, "pair", 0))):
        for which, piece in spread_over_tile(part):
            cots = lax.dynamic_update_slice(cots, piece[:, None, None], (0, side, which, 0, 0))
    cots = cots.reshape(-1, order)

    rows_index = tok_index * state_rows
    local_eye = jnp.arange(order)[None, :] == rows_index + jnp.arange(state_rows)[:, None]
    diagonal = jnp.sum(jnp.where(local_eye[None], statistics[:, 0], 0.0), axis=1)
    remainder = diagonal - lax.reduce_precision(diagonal, 8, 7)
    extra = jnp.broadcast_to(remainder[:, None], (blocks, 16, order))
    pieces = jnp.concatenate([statistics[:, 0], extra], 1).astype(jnp.bfloat16)
    pieces, acts = lax.optimization_barrier((pieces, acts))
    arrived = exchange(pieces, "tok")
    identity = jnp.eye(order, dtype=jnp.float32)
    lost = jnp.sum(arrived[:, state_rows].astype(jnp.float32), axis=0)
    previous = arrived[:, :state_rows].reshape(order, order).astype(jnp.float32)
    previous = previous + identity * lost

    mine = lax.dot_general(
        acts, cots, (((0,), (0,)), ((), ())), preferred_element_type=jnp.float32
    ).astype(jnp.bfloat16)
    other = swapped(mine, "pair", 0)
    first = pair_index == 0
    gradient = jnp.concatenate([jnp.where(first, mine, other), jnp.where(first, other, mine)], 0)
    wide = gradient.astype(jnp.float32)
    grad_sq = jnp.sum(wide * wide)
    factor_data = jnp.where(first, gradient, gradient.T)
    product = lax.dot_general(
        factor_data, factor_data, (((1,), (1,)), ((), ())), preferred_element_type=jnp.float32
    )
    product = lax.optimization_barrier(product)
    row_pieces = product.astype(jnp.bfloat16).reshape(blocks, state_rows, order)
    updated = 0.9 * previous + 0.1 * product
    identity = jnp.eye(order, dtype=jnp.float32)
    bound_max = jnp.max(jnp.sum(jnp.abs(updated), axis=1))
    iterate = ((updated + 0.1 * bound_max * identity) / (1.1 * bound_max)).astype(jnp.bfloat16)
    iterate = lax.optimization_barrier(iterate)
    root = iterate
    for iteration in range(ITERS):
        factor = ((5.0 * identity - iterate.astype(jnp.float32)) / 4.0).astype(jnp.bfloat16)
        root = factor if iteration == 0 else dot_bf(root, factor)
        if iteration + 1 < ITERS:
            square = dot_bf(factor, factor)
            fourth = dot_bf(square, square)
            iterate = lax.optimization_barrier(dot_bf(fourth, iterate))
    rows, partner = transfer(row_pieces, root, 0)
    left = jnp.where(first, root, partner)
    right = jnp.where(first, partner, root)
    left = left.reshape(blocks, 2, -1, order)
    left_rows = lax.dynamic_index_in_dim(left, pair_index, 1, keepdims=False).reshape(-1, order)
    left_mixed = dot_bf(left_rows, gradient)
    raw = jnp.dot(left_mixed, right, preferred_element_type=jnp.float32)
    local_sq = jnp.broadcast_to(jnp.sum(raw * raw), (8, 128))
    update_sq = (local_sq + swapped(local_sq, "pair", 0))[0, 0]
    update = (raw * jnp.sqrt(grad_sq / (update_sq + 1e-06))).astype(jnp.bfloat16)
    new_rows = 0.9 * statistics + 0.1 * rows[:, None].astype(jnp.float32)
    return (transfer(update.reshape(blocks, -1, order), None, 1)[0], new_rows)


def per_device(inputs, output_grads, statistics):
    blocks, _, _, order = statistics.shape
    tok_size = lax.axis_size("tok")
    owners = (
        blocks == tok_size
        and tok_size == lax.axis_size("tile")
        and tok_size & (tok_size - 1) == 0
        and lax.axis_size("pair") == 2
        and inputs.shape[1] == order
        and inputs.shape[0] % tok_size == 0
    )
    plan = owner_plan if owners else general_plan
    return plan(inputs, output_grads, statistics)


def solution(mesh):
    placed = (
        P(("tok", "pair"), "tile"),
        P(("tok", "pair"), "tile"),
        P("tile", "pair", "tok", None),
    )
    return jax.shard_map(
        per_device,
        mesh=mesh,
        in_specs=placed,
        out_specs=(P("tile", ("tok", "pair"), None), P("tile", "pair", "tok", None)),
        check_vma=False,
    )
```

```python
import functools

import jax
import jax.numpy as jnp
from jax import lax
from jax.experimental import pallas as pl
from jax.experimental.pallas import tpu as pltpu
from jax.sharding import PartitionSpec as P

ITERS = 2


def swapped(shard, axis, stride):
    return lax.ppermute(shard, axis, [(i, i ^ 1 << stride) for i in range(lax.axis_size(axis))])


def product_bf(left_part, right_part):
    return jnp.einsum(
        "kab,kbc->kac", left_part, right_part, preferred_element_type=jnp.float32
    ).astype(jnp.bfloat16)


def general_plan(inputs, output_grads, statistics):
    blocks = statistics.shape[0]
    state_rows = statistics.shape[2]
    matrix_order = statistics.shape[3]
    tile_count = lax.axis_size("tile")
    model_width = inputs.shape[1] * tile_count
    per_side = model_width // matrix_order
    tok_index = lax.axis_index("tok")
    pair_index = lax.axis_index("pair")
    shard_index = tok_index * lax.axis_size("pair") + pair_index
    devices_block = lax.axis_size("tok") * lax.axis_size("pair")
    out_rows = matrix_order // devices_block
    activations, cotangents = (
        lax.all_gather(inputs, "tile", axis=1, tiled=True),
        lax.all_gather(output_grads, "tile", axis=1, tiled=True),
    )
    first_block = lax.axis_index("tile") * blocks
    left_list = []
    right_list = []
    for offset in range(blocks):
        block_id = first_block + offset
        left_list.append(
            lax.dynamic_slice_in_dim(
                activations, block_id // per_side * matrix_order, matrix_order, 1
            )
        )
        right_list.append(
            lax.dynamic_slice_in_dim(
                cotangents, block_id % per_side * matrix_order, matrix_order, 1
            )
        )
    left_acts = jnp.stack(left_list)
    right_cots = jnp.stack(right_list)
    grad_share = lax.psum_scatter(
        jnp.einsum("ktr,ktc->rkc", left_acts, right_cots, preferred_element_type=jnp.float32),
        ("tok", "pair"),
        scatter_dimension=0,
        tiled=True,
    )
    gradient = lax.all_gather(grad_share.astype(jnp.bfloat16), ("tok", "pair"), axis=0, tiled=True)
    grad_sq = jnp.einsum("rkc,rkc->k", gradient, gradient, preferred_element_type=jnp.float32)
    by_rows = jnp.transpose(gradient, (1, 0, 2))
    by_cols = jnp.transpose(gradient, (1, 2, 0))
    factor_data = jnp.where(pair_index == 0, by_rows, by_cols)
    identity = jnp.eye(matrix_order, dtype=jnp.float32)
    row_start = tok_index * state_rows
    previous = lax.all_gather(statistics[:, 0], "tok", axis=1, tiled=True)
    product = jnp.einsum(
        "kac,kbc->kab", factor_data, factor_data, preferred_element_type=jnp.float32
    )
    updated = 0.9 * previous + 0.1 * product
    new_rows = lax.dynamic_slice_in_dim(updated, row_start, state_rows, 1)
    bound_max = jnp.max(jnp.sum(jnp.abs(updated), axis=2), axis=1)[:, None, None]
    iterate = ((updated + 0.1 * bound_max * identity) / (1.1 * bound_max)).astype(jnp.bfloat16)
    iterate = lax.optimization_barrier(iterate)
    root_whole = iterate
    for iteration in range(ITERS):
        factor = ((5.0 * identity - iterate.astype(jnp.float32)) / 4.0).astype(jnp.bfloat16)
        if iteration == 0:
            root_whole = factor
        else:
            root_whole = product_bf(root_whole, factor)
        if iteration + 1 < ITERS:
            square = product_bf(factor, factor)
            fourth = product_bf(square, square)
            iterate = lax.optimization_barrier(product_bf(fourth, iterate))
    partner = swapped(root_whole, "pair", 0)
    left_whole = jnp.where(pair_index == 0, root_whole, partner)
    right_whole = jnp.where(pair_index == 0, partner, root_whole)
    left_part = lax.dynamic_slice_in_dim(left_whole, shard_index * out_rows, out_rows, 1)
    left_mixed = jnp.einsum(
        "kqr,rkc->kqc", left_part, gradient, preferred_element_type=jnp.float32
    ).astype(jnp.bfloat16)
    raw_update = jnp.einsum(
        "kqc,kcd->kqd", left_mixed, right_whole, preferred_element_type=jnp.float32
    )
    local_sq = jnp.sum(raw_update * raw_update, axis=(1, 2))
    update_total = lax.psum(local_sq, ("tok", "pair"))
    graft_ratio = jnp.sqrt(grad_sq / (update_total + 1e-06))
    update = (raw_update * graft_ratio[:, None, None]).astype(jnp.bfloat16)
    return (update, new_rows[:, None])


def dot_bf(left_part, right_part):
    return jnp.dot(left_part, right_part, preferred_element_type=jnp.float32).astype(jnp.bfloat16)


def exchange(pieces, axis):
    size = lax.axis_size(axis)
    index = lax.axis_index(axis)
    result = pieces
    for step in range(1, size):
        piece = lax.dynamic_index_in_dim(pieces, index ^ step, 0, keepdims=True)
        arrived = lax.ppermute(piece, axis, [(i, i ^ step) for i in range(size)])
        result = lax.dynamic_update_slice_in_dim(result, arrived, index ^ step, 0)
    return result


def cotangent_quarter(output_grads, tok_size):
    tok_index = lax.axis_index("tok")
    tile_index = lax.axis_index("tile")
    quarters = output_grads.reshape(tok_size, -1, output_grads.shape[1])
    held = jnp.zeros_like(quarters)
    for step in range(tok_size):
        pairs = [
            (tok * tok_size + tile, tile * tok_size + (tok + step) % tok_size)
            for tok in range(tok_size)
            for tile in range(tok_size)
        ]
        piece = lax.dynamic_index_in_dim(quarters, (tok_index + step) % tok_size, 0, keepdims=True)
        arrived = lax.ppermute(piece, ("tok", "tile"), pairs)
        source = (tile_index + tok_size - step) % tok_size
        held = lax.dynamic_update_slice_in_dim(held, arrived, source, 0)
    return held


def spread_over_tile(piece):
    index = lax.axis_index("tile")
    held = [(index, piece)]
    bit = lax.axis_size("tile").bit_length() - 2
    while bit >= 0:
        held += [(which ^ (1 << bit), swapped(part, "tile", bit)) for which, part in held]
        bit -= 1
    return held


def transfer_body(size, with_swap, *refs):
    if with_swap:
        pieces, whole, result, partner, send_sem, recv_sem, own_sem = refs
    else:
        pieces, result, send_sem, recv_sem, own_sem = refs
    me = lax.axis_index("tok")
    side = lax.axis_index("pair")
    targets = [{"tok": lax.rem(me + step, size)} for step in range(1, size)]
    if with_swap:
        targets.append({"pair": 1 - side})
    barrier = pltpu.get_barrier_semaphore()
    for target in targets:
        pl.semaphore_signal(barrier, inc=1, device_id=target, device_id_type=pl.DeviceIdType.MESH)
    pl.semaphore_wait(barrier, len(targets))
    copies = []
    for slot, target in enumerate(targets):
        to_pair = slot == size - 1
        copies.append(
            pltpu.make_async_remote_copy(
                src_ref=whole if to_pair else pieces.at[target["tok"]],
                dst_ref=partner if to_pair else result.at[me],
                send_sem=send_sem.at[slot],
                recv_sem=recv_sem.at[slot],
                device_id=target,
                device_id_type=pl.DeviceIdType.MESH,
            )
        )
        copies[-1].start()
    own = pltpu.make_async_copy(pieces.at[me], result.at[me], own_sem)
    own.start()
    own.wait()
    for copy in copies:
        copy.wait()


def transfer(pieces, whole, collective_id):
    size = lax.axis_size("tok")
    arrays = [pieces] if whole is None else [pieces, whole]
    slots = size - 1 + (whole is not None)
    anywhere = pl.BlockSpec(memory_space=pl.ANY)
    return pl.pallas_call(
        functools.partial(transfer_body, size, whole is not None),
        out_shape=[jax.ShapeDtypeStruct(array.shape, array.dtype) for array in arrays],
        in_specs=[anywhere] * len(arrays),
        out_specs=[anywhere] * len(arrays),
        scratch_shapes=[
            pltpu.SemaphoreType.DMA((slots,)),
            pltpu.SemaphoreType.DMA((slots,)),
            pltpu.SemaphoreType.DMA,
        ],
        compiler_params=pltpu.CompilerParams(collective_id=collective_id, has_side_effects=True),
    )(*arrays)


def owner_plan(inputs, output_grads, statistics):
    blocks, _, state_rows, order = statistics.shape
    tok_index = lax.axis_index("tok")
    pair_index = lax.axis_index("pair")
    half = order // 2
    quarter = inputs.shape[0] // blocks
    held = cotangent_quarter(output_grads, blocks)
    acts_mine = lax.dynamic_slice_in_dim(inputs, pair_index * half, half, 1)
    acts_given = lax.dynamic_slice_in_dim(inputs, (1 - pair_index) * half, half, 1)
    acts = jnp.concatenate([acts_mine, swapped(acts_given, "pair", 0)], 0)
    acts, held = lax.optimization_barrier((acts, held))
    acts = lax.all_gather(acts, "tok", axis=0, tiled=True)
    cots = jnp.zeros((blocks, 2, blocks, quarter, order), output_grads.dtype)
    for side, part in enumerate((held, swapped(held, "pair", 0))):
        for which, piece in spread_over_tile(part):
            cots = lax.dynamic_update_slice(cots, piece[:, None, None], (0, side, which, 0, 0))
    cots = cots.reshape(-1, order)

    rows_index = tok_index * state_rows
    local_eye = jnp.arange(order)[None, :] == rows_index + jnp.arange(state_rows)[:, None]
    diagonal = jnp.sum(jnp.where(local_eye[None], statistics[:, 0], 0.0), axis=1)
    remainder = diagonal - lax.reduce_precision(diagonal, 8, 7)
    extra = jnp.broadcast_to(remainder[:, None], (blocks, 16, order))
    pieces = jnp.concatenate([statistics[:, 0], extra], 1).astype(jnp.bfloat16)
    doubled = jnp.concatenate([pieces, pieces], 2)
    pieces = lax.dynamic_slice_in_dim(doubled, rows_index, order - state_rows, 2)
    pieces, acts = lax.optimization_barrier((pieces, acts))
    arrived = exchange(pieces, "tok")
    identity = jnp.eye(order, dtype=jnp.float32)
    lost = arrived[:, state_rows, :state_rows].reshape(order).astype(jnp.float32)
    strips = arrived[:, :state_rows].reshape(blocks, state_rows, blocks - 1, state_rows)

    def block_at(row, column):
        ahead = (column - row) % blocks
        return strips[row, :, ahead] if ahead < blocks - 1 else strips[column, :, 1].T

    previous = jnp.block(
        [[block_at(row, column) for column in range(blocks)] for row in range(blocks)]
    ).astype(jnp.float32)
    previous = previous + identity * lost

    mine = lax.dot_general(
        acts, cots, (((0,), (0,)), ((), ())), preferred_element_type=jnp.float32
    ).astype(jnp.bfloat16)
    other = swapped(mine, "pair", 0)
    first = pair_index == 0
    gradient = jnp.concatenate([jnp.where(first, mine, other), jnp.where(first, other, mine)], 0)
    wide = gradient.astype(jnp.float32)
    grad_sq = jnp.sum(wide * wide)
    factor_data = jnp.where(first, gradient, gradient.T)
    product = lax.dot_general(
        factor_data, factor_data, (((1,), (1,)), ((), ())), preferred_element_type=jnp.float32
    )
    product = lax.optimization_barrier(product)
    row_pieces = product.astype(jnp.bfloat16).reshape(blocks, state_rows, order)
    updated = 0.9 * previous + 0.1 * product
    identity = jnp.eye(order, dtype=jnp.float32)
    bound_max = jnp.max(jnp.sum(jnp.abs(updated), axis=1))
    iterate = ((updated + 0.1 * bound_max * identity) / (1.1 * bound_max)).astype(jnp.bfloat16)
    iterate = lax.optimization_barrier(iterate)
    root = iterate
    for iteration in range(ITERS):
        factor = ((5.0 * identity - iterate.astype(jnp.float32)) / 4.0).astype(jnp.bfloat16)
        root = factor if iteration == 0 else dot_bf(root, factor)
        if iteration + 1 < ITERS:
            square = dot_bf(factor, factor)
            fourth = dot_bf(square, square)
            iterate = lax.optimization_barrier(dot_bf(fourth, iterate))
    rows, partner = transfer(row_pieces, root, 0)
    left = jnp.where(first, root, partner)
    right = jnp.where(first, partner, root)
    left = left.reshape(blocks, 2, -1, order)
    left_rows = lax.dynamic_index_in_dim(left, pair_index, 1, keepdims=False).reshape(-1, order)
    left_mixed = dot_bf(left_rows, gradient)
    raw = jnp.dot(left_mixed, right, preferred_element_type=jnp.float32)
    local_sq = jnp.broadcast_to(jnp.sum(raw * raw), (8, 128))
    update_sq = (local_sq + swapped(local_sq, "pair", 0))[0, 0]
    update = (raw * jnp.sqrt(grad_sq / (update_sq + 1e-06))).astype(jnp.bfloat16)
    new_rows = 0.9 * statistics + 0.1 * rows[:, None].astype(jnp.float32)
    return (transfer(update.reshape(blocks, -1, order), None, 1)[0], new_rows)


def per_device(inputs, output_grads, statistics):
    blocks, _, _, order = statistics.shape
    tok_size = lax.axis_size("tok")
    owners = (
        blocks == tok_size
        and tok_size > 2
        and statistics.shape[2] * tok_size == order
        and tok_size == lax.axis_size("tile")
        and tok_size & (tok_size - 1) == 0
        and lax.axis_size("pair") == 2
        and inputs.shape[1] == order
        and inputs.shape[0] % tok_size == 0
    )
    plan = owner_plan if owners else general_plan
    return plan(inputs, output_grads, statistics)


def solution(mesh):
    placed = (
        P(("tok", "pair"), "tile"),
        P(("tok", "pair"), "tile"),
        P("tile", "pair", "tok", None),
    )
    return jax.shard_map(
        per_device,
        mesh=mesh,
        in_specs=placed,
        out_specs=(P("tile", ("tok", "pair"), None), P("tile", "pair", "tok", None)),
        check_vma=False,
    )
```
